768 devices in a mesh: dp: 12 (over z_hi, x), tensor: 64 (over y, z_lo, core).
Axes of the slice: x: 4, y: 8, z: 12 (z_hi: 3, z_lo: 4; z = z_hi * 4 + z_lo), core: 2. Of those that a mesh axis runs over, the one named last changes fastest.
Arguments:
- out_grad: bfloat16 [6144, 6144], P(('dp', 'tensor')), may hold values from -24 to 24
- normed: bfloat16 [6144, 8192], P('dp', 'tensor'), may hold values from -0.078125 to 0.078125
- w_out: bfloat16 [8192, 6144], P('tensor', 'dp'), may hold values from -0.078125 to 0.078125
Outputs:
- d_normed: bfloat16 [6144, 8192], P('dp', 'tensor')
- d_w_out: bfloat16 [8192, 6144], P('tensor', 'dp')
The draws below stay inside these ranges and needn't reach their ends.
All inputs are finite; a program needn't handle non-finite values.
Results may differ from the reference program's by a relative error of at most 0.017.
Values may be sent and summed in bfloat16 or wider, within the bound.
A program may use at most 32 MiB of HBM per device.

```python
import jax
import jax.numpy as jnp
from jax import lax

D = 6144
INNER = 8192
ROWS_DP = 512
TOKENS = 6144
N_DP = 12


def strengthened(array, own_key, source, target, blocks, factor):
    def block_of(position):
        return (jnp.arange(array.shape[position]) // (array.shape[position] // blocks)).reshape((-1,) + (1,) * (array.ndim - 1 - position))

    near = jax.random.permutation(own_key, blocks)[block_of(target)]
    second = (block_of(target) + blocks // 2) % blocks
    return jnp.where((block_of(source) == near) | (block_of(source) == second), factor * array, array)


def level_of(key, dims, shards, smallest, largest):
    def one(position, shards_of):
        draws = jax.random.uniform(jax.random.fold_in(jax.random.fold_in(key, 6), position), (shards_of,), jnp.float32, smallest / len(shards), largest / len(shards))
        return jnp.repeat(jnp.exp(draws), dims[position] // shards_of).reshape((-1,) + (1,) * (len(dims) - position - 1))

    gain = one(*shards[0])
    for cut in shards[1:]:
        gain = gain * one(*cut)
    return gain


def bell_draw(own_key, extent, scale, bound, cuts=(), kind=jnp.bfloat16):
    values = scale * jax.random.normal(own_key, extent, jnp.float32)
    if cuts:
        values = values * level_of(own_key, extent, cuts, -0.22, 0.18)
    return jnp.clip(values, -bound, bound).astype(kind)


def noise_with(stream_key, shape, deviation, most, cuts, heavy, dtype=jnp.bfloat16):
    drawn = deviation * jax.random.normal(stream_key, shape, jnp.float32)
    if cuts:
        drawn = drawn * level_of(stream_key, shape, cuts, -0.22, 0.18)
    return jnp.clip(strengthened(drawn, jax.random.fold_in(stream_key, 3), *heavy), -most, most).astype(dtype)


def setup_inputs(seed: int = 0) -> dict:
    key_list = jax.random.split(jax.random.key(seed), 4)
    out_grad = noise_with(key_list[0], (TOKENS, D), 1.0, 24.0, ((0, 768),), (0, 1, 768, 6.0))
    normed = bell_draw(key_list[1], (TOKENS, INNER), TOKENS ** -0.5, 0.078125, ((0, 12), (1, 64)))
    w_out = bell_draw(key_list[2], (INNER, D), D ** -0.5, 0.078125, ((0, 64), (1, 12)))
    return dict(out_grad=out_grad, normed=normed, w_out=w_out)


def reference(out_grad, normed, w_out):
    d_normed = lax.dot_general(out_grad, w_out, (((1,), (1,)), ((), ())), preferred_element_type=jnp.float32).astype(jnp.bfloat16)
    grad_slices = out_grad.reshape(N_DP, ROWS_DP, D)
    norm_slices = normed.reshape(N_DP, ROWS_DP, INNER)

    def accumulate(total, pair):
        grad_rows, norm_rows = pair
        partial_value = lax.dot_general(norm_rows, grad_rows, (((0,), (0,)), ((), ())), preferred_element_type=jnp.float32)
        rounded = lax.optimization_barrier(partial_value.astype(jnp.bfloat16))
        return total + rounded.astype(jnp.float32), None

    total, unused = lax.scan(accumulate, jnp.zeros((INNER, D), jnp.float32), (grad_slices, norm_slices))
    return d_normed, total.astype(jnp.bfloat16)
```

```python
import jax
import jax.numpy as jnp
from jax import lax
from jax.experimental import pallas as pl
from jax.experimental.pallas import tpu as pltpu
from jax.sharding import PartitionSpec as P

X, ZH, Y, ZL = 4, 3, 8, 4
R = 8
C = 128
K = 2 * ZH
KZ = 2 * (ZH - 1)
W = X * C
B = 2 * R * ZL
RT = B * Y
LS, SS = Y // 2, Y // 2 - 1
WLAG = 2
MESH = pl.DeviceIdType.MESH
BF, F32 = jnp.bfloat16, jnp.float32


def kernel(
    og_ref, n_ref, w_ref, dn_ref, dw_ref,
    og_par, og, nb, nt, w, part, rsx, zs, rsz, fin, finr, acc, dns, dnr,
    c_send, c_recv, zl_send, zl_recv, y_send, y_recv, wz_send, wz_recv, wx_send, wx_recv,
    rsx_send, rsx_recv, rsz_send, rsz_recv,
):
    dp, tn = lax.axis_index("dp"), lax.axis_index("tensor")
    zh, x = dp // X, dp % X
    y, zl, c = tn // (2 * ZL), (tn // 2) % ZL, tn % 2
    o = 1 - c
    partner = (dp, tn + 1 - 2 * c)
    zl_peer = [(dp, (y * ZL + (zl + j) % ZL) * 2 + c) for j in range(1, ZL)]
    x_peer = [(zh * X + (x + j) % X, tn) for j in range(1, X)]
    z_peer = [(((zh + j) % ZH) * X + x, tn) for j in range(1, ZH)]

    def y_peer(sign):
        return (dp, (((y + sign + Y) % Y) * ZL + zl) * 2 + c)

    def send(src, dst, ssem, rsem, to):
        pltpu.make_async_remote_copy(
            src_ref=src, dst_ref=dst, send_sem=ssem, recv_sem=rsem, device_id=to, device_id_type=MESH
        ).start()

    def wait(ref, sem):
        pltpu.make_async_copy(ref, ref, sem).wait()

    def rows(k, start, size):
        return pl.ds(pl.multiple_of(k * RT + start, 16), size)

    def block(k, at):
        return og.at[rows(k, ((at + 2 * Y) % Y) * B, B)]

    def way(k):
        return 1 - 2 * (k % 2)

    def send_long(k, s):
        b = block(k, y - way(k) * s)
        send(b, b, y_send.at[k], y_recv.at[k, s], y_peer(way(k)))

    def send_short(k, s):
        b = block(k, y + way(k) * s)
        send(b, b, y_send.at[k], y_recv.at[k, LS + s], y_peer(-way(k)))

    def wait_long(k, s):
        wait(block(k, y - way(k) * (s + 1)), y_recv.at[k, s])

    def wait_short(k, s):
        wait(block(k, y + way(k) * (s + 1)), y_recv.at[k, LS + s])

    def send_w(k):
        for j in range(1, X):
            send(w.at[k, 0], w.at[k, X - j], wx_send.at[k], wx_recv.at[k], x_peer[j - 1])

    def weight(k):
        chunk = og[rows(k, 0, RT), :]
        p = jnp.dot(nt[...], chunk, preferred_element_type=F32)
        for j in range(X):
            part[k, j] = p[:, j * C : (j + 1) * C].astype(BF)
        for j in range(1, X):
            send(part.at[k, j], rsx.at[k, j - 1], rsx_send.at[k], rsx_recv.at[k], x_peer[j - 1])

    def summed(k):
        wait(rsx.at[k], rsx_recv.at[k])
        total = part[k, 0].astype(F32)
        for j in range(X - 1):
            total = total + rsx[k, j].astype(F32)
        return total

    def normed_grad(k):
        wait(w.at[k, pl.ds(1, X - 1)], wx_recv.at[k])
        chunk = og[rows(k, 0, RT), :]
        wk = jnp.concatenate([w[k, j] for j in range(X)], axis=1)
        acc[...] += lax.dot_general(chunk, wk, (((1,), (1,)), ((), ())), preferred_element_type=F32)

    barrier = pltpu.get_barrier_semaphore()
    peers = [partner] + zl_peer + x_peer + z_peer + [y_peer(1), y_peer(-1)]
    for peer in peers:
        pl.semaphore_signal(barrier, inc=1, device_id=peer, device_id_type=MESH)
    pl.semaphore_wait(barrier, len(peers))

    send(og_ref, og_par, c_send.at[0], c_recv.at[0], partner)
    mine = pl.ds(pl.multiple_of(c * C, C), C)
    for h in range(2):
        cols = pl.ds(pl.multiple_of(o * 2 * C + h * C, C), C)
        send(w_ref.at[:, cols], w.at[KZ + h, 0, mine], c_send.at[1 + h], c_recv.at[1 + h], partner)
    send(n_ref, nb.at[c], c_send.at[3], c_recv.at[3], partner)
    for h in range(2):
        w[KZ + h, 0, mine, :] = w_ref[:, pl.ds(pl.multiple_of(c * 2 * C + h * C, C), C)]
    nb[c] = n_ref[...]
    acc[...] = jnp.zeros_like(acc)

    slab = (y * ZL + zl) * 2 * R
    wait(og_par, c_recv.at[0])

    def spread(k, carry):
        zt = (zh + 1 + k // 2) % ZH
        for j in range(X):
            col = (zt * X + (x + j) % X) * 4 * C + c * 2 * C + (k % 2) * C
            col = pl.ds(pl.multiple_of(col, C), C)
            a, b = og_ref[:, col].astype(F32), og_par[:, col].astype(F32)
            top, low = jnp.where(c == 0, a, b), jnp.where(c == 0, b, a)
            og[rows(k, slab, 2 * R), j * C : (j + 1) * C] = jnp.concatenate([top, low], axis=0).astype(BF)
        piece = og.at[rows(k, slab, 2 * R)]
        for peer in zl_peer:
            send(piece, piece, zl_send.at[k], zl_recv.at[k], peer)
        return carry

    lax.fori_loop(0, K, spread, 0)

    for h in range(2):
        theirs = pl.ds(pl.multiple_of(o * C, C), C)
        wait(w.at[KZ + h, 0, theirs], c_recv.at[1 + h])
        for j in range(1, ZH):
            k = 2 * (ZH - 1 - j) + h
            send(w.at[KZ + h, 0], w.at[k, 0], wz_send.at[k], wz_recv.at[k], z_peer[j - 1])
    for h in range(2):
        send_w(KZ + h)
    wait(nb.at[o], c_recv.at[3])
    for i in range(2):
        nt[i * C : (i + 1) * C, :] = nb[i].astype(F32).T.astype(BF)

    def slot(s, carry):
        @pl.when(s < K)
        def _():
            wait(og.at[rows(s, 0, B - 2 * R)], zl_recv.at[s])
            send_long(s, 0)
            send_short(s, 0)

        for i in range(1, LS):
            @pl.when((s >= i) & (s - i < K))
            def _():
                k = s - i
                wait_long(k, i - 1)
                send_long(k, i)
                if i < SS:
                    wait_short(k, i - 1)
                    send_short(k, i)

        @pl.when((s >= WLAG) & (s - WLAG < KZ))
        def _():
            k = s - WLAG
            wait(w.at[k, 0], wz_recv.at[k])
            send_w(k)

        @pl.when(s >= LS)
        def _():
            k = s - LS
            wait_long(k, LS - 1)
            wait_short(k, SS - 1)
            weight(k)

        @pl.when(s >= LS + 1)
        def _():
            k = s - LS - 1
            zs[k] = summed(k).astype(BF)
            for i in range(ZH - 1):
                @pl.when(k // 2 == i)
                def _():
                    send(zs.at[k], rsz.at[k], rsz_send.at[k], rsz_recv.at[k], z_peer[i])
            normed_grad(k)

        return carry

    lax.fori_loop(0, K + LS - 1, slot, 0)

    def own(h):
        k = KZ + h
        total = summed(k)
        for i in range(ZH - 1):
            wait(rsz.at[2 * i + h], rsz_recv.at[2 * i + h])
            total = total + rsz[2 * i + h].astype(F32)
        part[k, 0] = total.astype(BF)
        theirs = pl.ds(pl.multiple_of(o * C, C), C)
        fin[h] = part[k, 0, theirs, :]
        send(fin.at[h], finr.at[h], c_send.at[4 + h], c_recv.at[4 + h], partner)
        dw_ref[:, pl.ds(pl.multiple_of(c * 2 * C + h * C, C), C)] = part[k, 0, mine, :]

    wait_long(K - 1, LS - 1)
    wait_short(K - 1, SS - 1)
    weight(K - 1)
    own(0)
    normed_grad(K - 2)
    normed_grad(K - 1)
    dns[...] = acc[:, pl.ds(pl.multiple_of(o * C, C), C)].astype(BF)
    send(dns, dnr, c_send.at[6], c_recv.at[6], partner)
    own(1)
    wait(dnr, c_recv.at[6])
    dn_ref[...] = (acc[:, mine] + dnr[...].astype(F32)).astype(BF)
    for h in range(2):
        wait(finr.at[h], c_recv.at[4 + h])
        dw_ref[:, pl.ds(pl.multiple_of(o * 2 * C + h * C, C), C)] = finr[h]

    wait(og_par, c_send.at[0])
    for h in range(2):
        wait(fin.at[h], c_send.at[1 + h])
        wait(fin.at[h], c_send.at[4 + h])
    wait(nb.at[0], c_send.at[3])
    wait(dns, c_send.at[6])

    def drain(k, carry):
        wait(og.at[rows(0, 0, (ZL - 1) * 2 * R)], zl_send.at[k])
        wait(og.at[rows(0, 0, (Y - 1) * B)], y_send.at[k])
        wait(rsx.at[k], wx_send.at[k])
        wait(rsx.at[k], rsx_send.at[k])
        return carry

    def drain_z(k, carry):
        wait(zs.at[k], wz_send.at[k])
        wait(zs.at[k], rsz_send.at[k])
        return carry

    lax.fori_loop(0, K, drain, 0)
    lax.fori_loop(0, KZ, drain_z, 0)


def body(out_grad, normed, w_out):
    dma = pltpu.SemaphoreType.DMA
    vmem = pl.BlockSpec(memory_space=pltpu.VMEM)
    return pl.pallas_call(
        kernel,
        out_shape=(jax.ShapeDtypeStruct((RT, C), BF), jax.ShapeDtypeStruct((C, 4 * C), BF)),
        in_specs=[vmem] * 3,
        out_specs=(vmem, vmem),
        scratch_shapes=[
            pltpu.VMEM((R, ZH * X * 4 * C), BF),
            pltpu.VMEM((K * RT, W), BF),
            pltpu.VMEM((2, RT, C), BF),
            pltpu.VMEM((2 * C, RT), BF),
            pltpu.VMEM((K, X, 2 * C, C), BF),
            pltpu.VMEM((K, X, 2 * C, C), BF),
            pltpu.VMEM((K, X - 1, 2 * C, C), BF),
            pltpu.VMEM((KZ, 2 * C, C), BF),
            pltpu.VMEM((KZ, 2 * C, C), BF),
            pltpu.VMEM((2, C, C), BF),
            pltpu.VMEM((2, C, C), BF),
            pltpu.VMEM((RT, 2 * C), F32),
            pltpu.VMEM((RT, C), BF),
            pltpu.VMEM((RT, C), BF),
            dma((7,)), dma((7,)),
            dma((K,)), dma((K,)),
            dma((K,)), dma((K, LS + SS)),
            dma((KZ,)), dma((KZ,)),
            dma((K,)), dma((K,)),
            dma((K,)), dma((K,)),
            dma((KZ,)), dma((KZ,)),
        ],
        compiler_params=pltpu.CompilerParams(
            collective_id=0, has_side_effects=True, vmem_limit_bytes=40 * 1024 * 1024
        ),
        cost_estimate=pl.CostEstimate(flops=1_600_000_000, bytes_accessed=1_000_000, transcendentals=0),
    )(out_grad, normed, w_out)


def solution(mesh):
    in_specs = (P(("dp", "tensor"), None), P("dp", "tensor"), P("tensor", "dp"))
    out_specs = (P("dp", "tensor"), P("tensor", "dp"))
    return jax.shard_map(body, mesh=mesh, in_specs=in_specs, out_specs=out_specs, check_vma=False)
```

```python
import jax
import jax.numpy as jnp
from jax import lax
from jax.experimental import pallas as pl
from jax.experimental.pallas import tpu as pltpu
from jax.sharding import PartitionSpec as P

X, ZH, Y, ZL = 4, 3, 8, 4
R = 8
C = 128
W = 2 * C
OWN = ZH - 1
B = 2 * R * ZL
RT = B * Y
LS, SS = Y // 2, Y // 2 - 1
FAR, SIDES, TWICE, HERE = 0, 1, 2, 3
ORDER = [
    (0, FAR, 0), (1, FAR, 0), (0, SIDES, 0), (1, SIDES, 0), (0, FAR, 1), (1, FAR, 1),
    (0, SIDES, 1), (1, SIDES, 1), (2, TWICE, 0), (2, SIDES, 0), (2, SIDES, 1), (2, HERE, 0),
]
K = len(ORDER)
G_TABLE = sum(g << (2 * i) for i, (g, kind, h) in enumerate(ORDER))
KIND_TABLE = sum(kind << (2 * i) for i, (g, kind, h) in enumerate(ORDER))
H_TABLE = sum(h << i for i, (g, kind, h) in enumerate(ORDER))
Z_SLOTS = [(4, 0, 0), (5, 1, 0), (8, 0, 1), (9, 1, 1)]
GROUPS = [(0, 1), (1, 1), (2, 2), (4, 4), (8, 4)]
HOP = 3
LEAD = 1
W_START, W_OWN, W_Z, W_FAR, W_ALL = 7, 12, 17, 22, 25
NG_FROM, NG_RATE = 7, 3
MESH = pl.DeviceIdType.MESH
BF, F32 = jnp.bfloat16, jnp.float32


def pieces(kind, h):
    return {FAR: ((2, h), (0, h)), SIDES: ((1, h), (3, h)), TWICE: ((2, 0), (2, 1)), HERE: ((0, 0), (0, 1))}[kind]


def kernel(
    og_ref, n_ref, w_ref, dn_ref, dw_ref,
    og_own, og_par, og, nb, nt, w, part, kept, rsh, rsx, zs, rsz, fin, finr, acc, dns, dnr,
    own_sem, c_send, c_recv, zl_send, zl_recv, y_send, y_recv, wz_send, wz_recv, wx_send, wx_recv,
    rs_send, rsh_recv, rsx_recv, rsz_send, rsz_recv,
):
    dp, tn = lax.axis_index("dp"), lax.axis_index("tensor")
    zh, x = dp // X, dp % X
    y, zl, c = tn // (2 * ZL), (tn // 2) % ZL, tn % 2
    o = 1 - c
    partner = (dp, tn + 1 - 2 * c)
    zl_peer = [(dp, (y * ZL + (zl + j) % ZL) * 2 + c) for j in range(1, ZL)]
    z_peer = [(((zh + j) % ZH) * X + x, tn) for j in range(1, ZH)]
    x_up, x_down = (zh * X + (x + 1) % X, tn), (zh * X + (x + X - 1) % X, tn)

    def y_peer(sign):
        return (dp, (((y + sign + Y) % Y) * ZL + zl) * 2 + c)

    def send(src, dst, ssem, rsem, to):
        pltpu.make_async_remote_copy(
            src_ref=src, dst_ref=dst, send_sem=ssem, recv_sem=rsem, device_id=to, device_id_type=MESH
        ).start()

    def wait(ref, sem):
        pltpu.make_async_copy(ref, ref, sem).wait()

    mine, theirs = pl.ds(pl.multiple_of(c * C, C), C), pl.ds(pl.multiple_of(o * C, C), C)
    upper, lower = pl.ds(0, C), pl.ds(C, C)

    def half(of, h):
        return pl.ds(pl.multiple_of(of * W + h * C, C), C)

    stays = [
        pltpu.make_async_copy(og_ref, og_own, own_sem.at[0]),
        pltpu.make_async_copy(w_ref.at[:, half(c, 0)], w.at[OWN, 0, 0, mine], own_sem.at[1]),
        pltpu.make_async_copy(w_ref.at[:, half(c, 1)], w.at[OWN, 0, 1, mine], own_sem.at[2]),
        pltpu.make_async_copy(n_ref, nb.at[c], own_sem.at[3]),
    ]
    for copy in stays:
        copy.start()

    barrier = pltpu.get_barrier_semaphore()
    peers = [partner] + zl_peer + [x_up, x_down] + z_peer + [y_peer(1), y_peer(-1)]
    for peer in peers:
        pl.semaphore_signal(barrier, inc=1, device_id=peer, device_id_type=MESH)
    acc[...] = jnp.zeros_like(acc)
    pl.semaphore_wait(barrier, len(peers))

    send(og_ref, og_par, c_send.at[0], c_recv.at[0], partner)
    for h in range(2):
        send(w_ref.at[:, half(o, h)], w.at[OWN, 0, h, mine], c_send.at[5 + h], c_recv.at[5 + h], partner)
    send(n_ref, nb.at[c], c_send.at[2], c_recv.at[2], partner)

    slab = pl.ds(pl.multiple_of((y * ZL + zl) * 2 * R, 2 * R), 2 * R)
    stays[0].wait()
    wait(og_par, c_recv.at[0])
    for q, (first, number) in enumerate(GROUPS):
        for k in range(first, first + number):
            g, kind, h = ORDER[k]
            for i, (j, h) in enumerate(pieces(kind, h)):
                col = ((zh + 1 + g) % ZH * X + (x + j) % X) * 2 * W + c * W + h * C
                col = pl.ds(pl.multiple_of(col, C), C)
                a, b = og_own[:, col].astype(F32), og_par[:, col].astype(F32)
                top, low = jnp.where(c == 0, a, b), jnp.where(c == 0, b, a)
                og[k, slab, i * C : (i + 1) * C] = jnp.concatenate([top, low], axis=0).astype(BF)
        piece = og.at[pl.ds(first, number), slab]
        for peer in zl_peer:
            send(piece, piece, zl_send.at[q], zl_recv.at[q], peer)

    def w_start():
        for h in range(2):
            stays[1 + h].wait()
            wait(w.at[OWN, 0, h, theirs], c_recv.at[5 + h])
        w_near(OWN)
        for j in range(1, ZH):
            g = ZH - 1 - j
            send(w.at[OWN, 0], w.at[g, 0], wz_send.at[g], wz_recv.at[g], z_peer[j - 1])

    def w_near(g):
        send(w.at[g, 0], w.at[g, 3], wx_send.at[g, 0], wx_recv.at[g, 0], x_up)
        send(w.at[g, 0], w.at[g, 1], wx_send.at[g, 1], wx_recv.at[g, 1], x_down)

    def w_far(g):
        wait(w.at[g, 3], wx_recv.at[g, 0])
        send(w.at[g, 3, :, upper], w.at[g, 2, :, upper], wx_send.at[g, 2], wx_recv.at[g, 2], x_up)
        wait(w.at[g, 1], wx_recv.at[g, 1])
        send(w.at[g, 1, :, lower], w.at[g, 2, :, lower], wx_send.at[g, 3], wx_recv.at[g, 3], x_down)

    def block(k, at):
        return og.at[k, pl.ds(pl.multiple_of(((at + 2 * Y) % Y) * B, B), B)]

    def way(k):
        return 1 - 2 * (k % 2)

    def send_long(k, s):
        b = block(k, y - way(k) * s)
        send(b, b, y_send.at[k], y_recv.at[k, s], y_peer(way(k)))

    def send_short(k, s):
        b = block(k, y + way(k) * s)
        send(b, b, y_send.at[k], y_recv.at[k, LS + s], y_peer(-way(k)))

    def wait_long(k, s):
        wait(block(k, y - way(k) * (s + 1)), y_recv.at[k, s])

    def wait_short(k, s):
        wait(block(k, y + way(k) * (s + 1)), y_recv.at[k, LS + s])

    def begin(k):
        for q, (first, number) in enumerate(GROUPS):
            @pl.when(k == first)
            def _():
                wait(og.at[pl.ds(first, number), pl.ds(0, B - 2 * R)], zl_recv.at[q])

        send_long(k, 0)
        send_short(k, 0)

    def gathered(k):
        wait_long(k, LS - 1)
        wait_short(k, SS - 1)

    def chunk_weight(k):
        return jnp.dot(nt[...], og[k], preferred_element_type=F32)

    def x_sum(g, h, total):
        for i in range(2):
            wait(rsx.at[g, h, i], rsx_recv.at[g, h, i])
            total = total + rsx[g, h, i].astype(F32)
        return total

    def weight(k):
        g, kind, h = (G_TABLE >> (2 * k)) & 3, (KIND_TABLE >> (2 * k)) & 3, (H_TABLE >> k) & 1
        p = chunk_weight(k)

        def far(h):
            send(part.at[k, h, upper], rsh.at[g, h, 0], rs_send.at[g, h, 0], rsh_recv.at[g, h, 0], x_up)
            send(part.at[k, h, lower], rsh.at[g, h, 1], rs_send.at[g, h, 1], rsh_recv.at[g, h, 1], x_down)

        @pl.when(kind == FAR)
        def _():
            part[k, h] = p[:, :C].astype(BF)
            far(h)
            kept[g, h] = p[:, C:]

        @pl.when(kind == TWICE)
        def _():
            for i in range(2):
                part[k, i] = p[:, i * C : (i + 1) * C].astype(BF)
            for i in range(2):
                far(i)

        @pl.when(kind == SIDES)
        def _():
            wait(rsh.at[g, h, 0], rsh_recv.at[g, h, 0])
            part[k, 0, :C] = (p[:C, :C] + rsh[g, h, 0].astype(F32)).astype(BF)
            part[k, 0, C:] = p[C:, :C].astype(BF)
            send(part.at[k, 0], rsx.at[g, h, 0], rs_send.at[g, h, 2], rsx_recv.at[g, h, 0], x_up)
            wait(rsh.at[g, h, 1], rsh_recv.at[g, h, 1])
            part[k, 1, :C] = p[:C, C:].astype(BF)
            part[k, 1, C:] = (p[C:, C:] + rsh[g, h, 1].astype(F32)).astype(BF)
            send(part.at[k, 1], rsx.at[g, h, 1], rs_send.at[g, h, 3], rsx_recv.at[g, h, 1], x_down)

        for at, gz, hz in Z_SLOTS:
            @pl.when(k == at)
            def _():
                zs[gz, hz] = x_sum(gz, hz, kept[gz, hz]).astype(BF)
                send(zs.at[gz, hz], rsz.at[gz, hz], rsz_send.at[gz, hz], rsz_recv.at[gz, hz], z_peer[gz])

    def normed_grad(k, carry):
        g, kind, h = (G_TABLE >> (2 * k)) & 3, (KIND_TABLE >> (2 * k)) & 3, (H_TABLE >> k) & 1
        ja = jnp.where(kind == SIDES, 1, jnp.where(kind == HERE, 0, 2))
        jb = jnp.where(kind == SIDES, 3, jnp.where(kind == TWICE, 2, 0))
        hb = jnp.where(kind >= TWICE, 1, h)
        wk = jnp.concatenate([w[g, ja, h], w[g, jb, hb]], axis=1)
        acc[...] += lax.dot_general(og[k], wk, (((1,), (1,)), ((), ())), preferred_element_type=F32)
        return carry

    def normed_to(k):
        return jnp.clip(NG_RATE * (k - NG_FROM) + 2, 0, k + 1)

    for k in range(LEAD):
        begin(k)

    def slot(s, carry):
        @pl.when((s % 2 == 0) & (s // 2 + LEAD < K))
        def _():
            begin(s // 2 + LEAD)

        for i in range(1, LS):
            k = (s - HOP * i) // 2

            @pl.when((s >= HOP * i) & ((s - HOP * i) % 2 == 0) & (k < K))
            def _(i=i, k=k):
                wait_long(k, i - 1)
                send_long(k, i)
                if i < SS:
                    wait_short(k, i - 1)
                    send_short(k, i)

        @pl.when(s == HOP * LS - 1)
        def _():
            stays[3].wait()
            wait(nb.at[o], c_recv.at[2])
            for i in range(2):
                nt[i * C : (i + 1) * C, :] = nb[i].astype(F32).T.astype(BF)

        @pl.when(s == W_START)
        def _():
            w_start()

        @pl.when(s == W_OWN)
        def _():
            w_far(OWN)

        @pl.when(s == W_Z)
        def _():
            for g in range(OWN):
                wait(w.at[g, 0], wz_recv.at[g])
                w_near(g)

        @pl.when(s == W_FAR)
        def _():
            for g in range(OWN):
                w_far(g)

        @pl.when(s == W_ALL)
        def _():
            for g in range(ZH):
                wait(w.at[g, 2, :, upper], wx_recv.at[g, 2])
                wait(w.at[g, 2, :, lower], wx_recv.at[g, 3])

        @pl.when((s >= HOP * LS) & ((s - HOP * LS) % 2 == 0))
        def _():
            k = (s - HOP * LS) // 2
            gathered(k)
            weight(k)
            lax.fori_loop(normed_to(k - 1), normed_to(k), normed_grad, 0)

        return carry

    lax.fori_loop(0, 2 * (K - 1) + HOP * LS, slot, 0)

    gathered(K - 1)
    lax.fori_loop(normed_to(K - 2), K, normed_grad, 0)
    dns[...] = acc[:, theirs].astype(BF)
    send(dns, dnr, c_send.at[4], c_recv.at[4], partner)
    p = chunk_weight(K - 1)
    for h in range(2):
        total = x_sum(OWN, h, p[:, h * C : (h + 1) * C])
        for i in range(OWN):
            wait(rsz.at[i, h], rsz_recv.at[i, h])
            total = total + rsz[i, h].astype(F32)
        part[K - 1, h] = total.astype(BF)
        fin[:, h * C : (h + 1) * C] = part[K - 1, h, theirs, :]
    send(fin, finr, c_send.at[3], c_recv.at[3], partner)
    for h in range(2):
        dw_ref[:, half(c, h)] = part[K - 1, h, mine, :]
    wait(dnr, c_recv.at[4])
    dn_ref[...] = (acc[:, mine] + dnr[...].astype(F32)).astype(BF)

    wait(og_par, c_send.at[0])
    for h in range(2):
        wait(w.at[OWN, 0, h, mine], c_send.at[5 + h])
    wait(nb.at[0], c_send.at[2])
    wait(fin, c_send.at[3])
    wait(dns, c_send.at[4])
    for q, (first, number) in enumerate(GROUPS):
        wait(og.at[pl.ds(first, number), pl.ds(0, (ZL - 1) * 2 * R)], zl_send.at[q])
    for g in range(OWN):
        wait(w.at[g, 0], wz_send.at[g])
        for h in range(2):
            wait(zs.at[g, h], rsz_send.at[g, h])
    for g in range(ZH):
        wait(w.at[g, 3], wx_send.at[g, 0])
        wait(w.at[g, 1], wx_send.at[g, 1])
        wait(w.at[g, 2, :, upper], wx_send.at[g, 2])
        wait(w.at[g, 2, :, lower], wx_send.at[g, 3])

    for g in range(ZH):
        for h in range(2):
            for i in range(2):
                wait(rsh.at[g, h, i], rs_send.at[g, h, i])
                wait(rsx.at[g, h, i], rs_send.at[g, h, 2 + i])

    def drain(k, carry):
        wait(og.at[k, pl.ds(0, (Y - 1) * B)], y_send.at[k])
        return carry

    lax.fori_loop(0, K, drain, 0)
    wait(finr, c_recv.at[3])
    dw_ref[:, pl.ds(pl.multiple_of(o * W, W), W)] = finr[...]


def body(out_grad, normed, w_out):
    dma = pltpu.SemaphoreType.DMA
    vmem, hbm = pl.BlockSpec(memory_space=pltpu.VMEM), pl.BlockSpec(memory_space=pl.ANY)
    cols = ZH * X * 2 * W
    return pl.pallas_call(
        kernel,
        out_shape=(jax.ShapeDtypeStruct((RT, C), BF), jax.ShapeDtypeStruct((C, 2 * W), BF)),
        in_specs=[hbm] * 3,
        out_specs=(vmem, vmem),
        scratch_shapes=[
            pltpu.VMEM((R, cols), BF),
            pltpu.VMEM((R, cols), BF),
            pltpu.VMEM((K, RT, W), BF),
            pltpu.VMEM((2, RT, C), BF),
            pltpu.VMEM((2 * C, RT), BF),
            pltpu.VMEM((ZH, X, 2, 2 * C, C), BF),
            pltpu.VMEM((K, 2, 2 * C, C), BF),
            pltpu.VMEM((OWN, 2, 2 * C, C), F32),
            pltpu.VMEM((ZH, 2, 2, C, C), BF),
            pltpu.VMEM((ZH, 2, 2, 2 * C, C), BF),
            pltpu.VMEM((OWN, 2, 2 * C, C), BF),
            pltpu.VMEM((OWN, 2, 2 * C, C), BF),
            pltpu.VMEM((C, W), BF),
            pltpu.VMEM((C, W), BF),
            pltpu.VMEM((RT, 2 * C), F32),
            pltpu.VMEM((RT, C), BF),
            pltpu.VMEM((RT, C), BF),
            dma((4,)), dma((7,)), dma((7,)),
            dma((len(GROUPS),)), dma((len(GROUPS),)),
            dma((K,)), dma((K, LS + SS)),
            dma((OWN,)), dma((OWN,)),
            dma((ZH, 4)), dma((ZH, 4)),
            dma((ZH, 2, 4)), dma((ZH, 2, 2)), dma((ZH, 2, 2)),
            dma((OWN, 2)), dma((OWN, 2)),
        ],
        compiler_params=pltpu.CompilerParams(
            collective_id=0, has_side_effects=True, vmem_limit_bytes=56 * 1024 * 1024
        ),
        cost_estimate=pl.CostEstimate(flops=1_600_000_000, bytes_accessed=1_000_000, transcendentals=0),
    )(out_grad, normed, w_out)


def solution(mesh):
    in_specs = (P(("dp", "tensor"), None), P("dp", "tensor"), P("tensor", "dp"))
    out_specs = (P("dp", "tensor"), P("tensor", "dp"))
    return jax.shard_map(body, mesh=mesh, in_specs=in_specs, out_specs=out_specs, check_vma=False)
```

```python
import jax
import jax.numpy as jnp
from jax import lax
from jax.experimental import pallas as pl
from jax.experimental.pallas import tpu as pltpu
from jax.sharding import PartitionSpec as P

X, ZH, Y, ZL = 4, 3, 8, 4
R = 8
C = 128
W = 2 * C
OWN = ZH - 1
B = 2 * R * ZL
RT = B * Y
LS, SS = Y // 2, Y // 2 - 1
FAR, SIDES, TWICE, HERE = 0, 1, 2, 3
ORDER = [
    (0, FAR, 0), (1, FAR, 0), (0, SIDES, 0), (1, SIDES, 0), (0, FAR, 1), (1, FAR, 1),
    (0, SIDES, 1), (1, SIDES, 1), (2, TWICE, 0), (2, SIDES, 0), (2, SIDES, 1), (2, HERE, 0),
]
K = len(ORDER)
G_TABLE = sum(g << (2 * i) for i, (g, kind, h) in enumerate(ORDER))
KIND_TABLE = sum(kind << (2 * i) for i, (g, kind, h) in enumerate(ORDER))
H_TABLE = sum(h << i for i, (g, kind, h) in enumerate(ORDER))
Z_SLOTS = [(4, 0, 0), (5, 1, 0), (8, 0, 1), (9, 1, 1)]
GROUPS = [(0, 1), (1, 1), (2, 2), (4, 4), (8, 4)]
HOP = 3
LEAD = 1
W_START, W_OWN, W_Z, W_FAR, W_ALL = 7, 12, 17, 22, 25
NG_FROM, NG_RATE = 7, 3
MESH = pl.DeviceIdType.MESH
BF, F32 = jnp.bfloat16, jnp.float32


def pieces(kind, h):
    return {FAR: ((2, h), (0, h)), SIDES: ((1, h), (3, h)), TWICE: ((2, 0), (2, 1)), HERE: ((0, 0), (0, 1))}[kind]


def kernel(
    og_ref, n_ref, w_ref, dn_ref, dw_ref,
    og_own, og_par, og, nb, nt, w, part, kept, rsh, rsx, zs, rsz, fin, finr, acc, dns, dnr,
    own_sem, c_send, c_recv, zl_send, zl_recv, y_send, y_recv, wz_send, wz_recv, wx_send, wx_recv,
    rs_send, rsh_recv, rsx_recv, rsz_send, rsz_recv,
):
    dp, tn = lax.axis_index("dp"), lax.axis_index("tensor")
    zh, x = dp // X, dp % X
    y, zl, c = tn // (2 * ZL), (tn // 2) % ZL, tn % 2
    o = 1 - c
    partner = (dp, tn + 1 - 2 * c)
    zl_peer = [(dp, (y * ZL + (zl + j) % ZL) * 2 + c) for j in range(1, ZL)]
    z_peer = [(((zh + j) % ZH) * X + x, tn) for j in range(1, ZH)]
    x_up, x_down = (zh * X + (x + 1) % X, tn), (zh * X + (x + X - 1) % X, tn)

    def y_peer(sign):
        return (dp, (((y + sign + Y) % Y) * ZL + zl) * 2 + c)

    def send(src, dst, ssem, rsem, to):
        pltpu.make_async_remote_copy(
            src_ref=src, dst_ref=dst, send_sem=ssem, recv_sem=rsem, device_id=to, device_id_type=MESH
        ).start()

    def wait(ref, sem):
        pltpu.make_async_copy(ref, ref, sem).wait()

    mine, theirs = pl.ds(pl.multiple_of(c * C, C), C), pl.ds(pl.multiple_of(o * C, C), C)
    upper, lower = pl.ds(0, C), pl.ds(C, C)

    def half(of, h):
        return pl.ds(pl.multiple_of(of * W + h * C, C), C)

    stays = [
        pltpu.make_async_copy(og_ref, og_own, own_sem.at[0]),
        pltpu.make_async_copy(w_ref.at[:, half(c, 0)], w.at[OWN, 0, 0, mine], own_sem.at[1]),
        pltpu.make_async_copy(w_ref.at[:, half(c, 1)], w.at[OWN, 0, 1, mine], own_sem.at[2]),
        pltpu.make_async_copy(n_ref, nb.at[c], own_sem.at[3]),
    ]
    for copy in stays:
        copy.start()

    barrier = pltpu.get_barrier_semaphore()
    peers = [partner] + zl_peer + [x_up, x_down] + z_peer + [y_peer(1), y_peer(-1)]
    for peer in peers:
        pl.semaphore_signal(barrier, inc=1, device_id=peer, device_id_type=MESH)
    acc[...] = jnp.zeros_like(acc)
    pl.semaphore_wait(barrier, len(peers))

    send(og_ref, og_par, c_send.at[0], c_recv.at[0], partner)
    for h in range(2):
        send(w_ref.at[:, half(o, h)], w.at[OWN, 0, h, mine], c_send.at[5 + h], c_recv.at[5 + h], partner)
    send(n_ref, nb.at[c], c_send.at[2], c_recv.at[2], partner)

    slab = pl.ds(pl.multiple_of((y * ZL + zl) * 2 * R, 2 * R), 2 * R)
    stays[0].wait()
    wait(og_par, c_recv.at[0])
    for q, (first, number) in enumerate(GROUPS):
        for k in range(first, first + number):
            g, kind, h = ORDER[k]
            for i, (j, h) in enumerate(pieces(kind, h)):
                col = ((zh + 1 + g) % ZH * X + (x + j) % X) * 2 * W + c * W + h * C
                col = pl.ds(pl.multiple_of(col, C), C)
                a, b = og_own[:, col].astype(F32), og_par[:, col].astype(F32)
                top, low = jnp.where(c == 0, a, b), jnp.where(c == 0, b, a)
                og[k, slab, i * C : (i + 1) * C] = jnp.concatenate([top, low], axis=0).astype(BF)
        piece = og.at[pl.ds(first, number), slab]
        for peer in zl_peer:
            send(piece, piece, zl_send.at[q], zl_recv.at[q], peer)

    def w_start():
        for h in range(2):
            stays[1 + h].wait()
            wait(w.at[OWN, 0, h, theirs], c_recv.at[5 + h])
        w_near(OWN)
        for j in range(1, ZH):
            g = ZH - 1 - j
            send(w.at[OWN, 0], w.at[g, 0], wz_send.at[g], wz_recv.at[g], z_peer[j - 1])

    def w_near(g):
        send(w.at[g, 0], w.at[g, 3], wx_send.at[g, 0], wx_recv.at[g, 0], x_up)
        send(w.at[g, 0], w.at[g, 1], wx_send.at[g, 1], wx_recv.at[g, 1], x_down)

    def w_far(g):
        wait(w.at[g, 3], wx_recv.at[g, 0])
        send(w.at[g, 3, :, upper], w.at[g, 2, :, upper], wx_send.at[g, 2], wx_recv.at[g, 2], x_up)
        wait(w.at[g, 1], wx_recv.at[g, 1])
        send(w.at[g, 1, :, lower], w.at[g, 2, :, lower], wx_send.at[g, 3], wx_recv.at[g, 3], x_down)

    def block(k, at):
        return og.at[k, pl.ds(pl.multiple_of(((at + 2 * Y) % Y) * B, B), B)]

    def way(k):
        return 1 - 2 * (k % 2)

    def send_long(k, s):
        b = block(k, y - way(k) * s)
        send(b, b, y_send.at[k], y_recv.at[k, s], y_peer(way(k)))

    def send_short(k, s):
        b = block(k, y + way(k) * s)
        send(b, b, y_send.at[k], y_recv.at[k, LS + s], y_peer(-way(k)))

    def wait_long(k, s):
        wait(block(k, y - way(k) * (s + 1)), y_recv.at[k, s])

    def wait_short(k, s):
        wait(block(k, y + way(k) * (s + 1)), y_recv.at[k, LS + s])

    def begin(k):
        for q, (first, number) in enumerate(GROUPS):
            @pl.when(k == first)
            def _():
                wait(og.at[pl.ds(first, number), pl.ds(0, B - 2 * R)], zl_recv.at[q])

        send_long(k, 0)
        send_short(k, 0)

    def gathered(k):
        wait_long(k, LS - 1)
        wait_short(k, SS - 1)

    def chunk_weight(k):
        return jnp.dot(nt[...], og[k], preferred_element_type=F32)

    def x_sum(g, h, total):
        for i in range(2):
            wait(rsx.at[g, h, i], rsx_recv.at[g, h, i])
            total = total + rsx[g, h, i].astype(F32)
        return total

    def weight(k):
        g, kind, h = (G_TABLE >> (2 * k)) & 3, (KIND_TABLE >> (2 * k)) & 3, (H_TABLE >> k) & 1
        p = chunk_weight(k)

        def far(h):
            send(part.at[k, h, upper], rsh.at[g, h, 0], rs_send.at[g, h, 0], rsh_recv.at[g, h, 0], x_up)
            send(part.at[k, h, lower], rsh.at[g, h, 1], rs_send.at[g, h, 1], rsh_recv.at[g, h, 1], x_down)

        @pl.when(kind == FAR)
        def _():
            part[k, h] = p[:, :C].astype(BF)
            far(h)
            kept[g, h] = p[:, C:]

        @pl.when(kind == TWICE)
        def _():
            for i in range(2):
                part[k, i] = p[:, i * C : (i + 1) * C].astype(BF)
            for i in range(2):
                far(i)

        @pl.when(kind == SIDES)
        def _():
            wait(rsh.at[g, h, 0], rsh_recv.at[g, h, 0])
            part[k, 0, :C] = (p[:C, :C] + rsh[g, h, 0].astype(F32)).astype(BF)
            part[k, 0, C:] = p[C:, :C].astype(BF)
            send(part.at[k, 0], rsx.at[g, h, 0], rs_send.at[g, h, 2], rsx_recv.at[g, h, 0], x_up)
            wait(rsh.at[g, h, 1], rsh_recv.at[g, h, 1])
            part[k, 1, :C] = p[:C, C:].astype(BF)
            part[k, 1, C:] = (p[C:, C:] + rsh[g, h, 1].astype(F32)).astype(BF)
            send(part.at[k, 1], rsx.at[g, h, 1], rs_send.at[g, h, 3], rsx_recv.at[g, h, 1], x_down)

        for at, gz, hz in Z_SLOTS:
            @pl.when(k == at)
            def _():
                zs[gz, hz] = x_sum(gz, hz, kept[gz, hz]).astype(BF)
                send(zs.at[gz, hz], rsz.at[gz, hz], rsz_send.at[gz, hz], rsz_recv.at[gz, hz], z_peer[gz])

    def normed_grad(k, carry):
        g, kind, h = (G_TABLE >> (2 * k)) & 3, (KIND_TABLE >> (2 * k)) & 3, (H_TABLE >> k) & 1
        ja = jnp.where(kind == SIDES, 1, jnp.where(kind == HERE, 0, 2))
        jb = jnp.where(kind == SIDES, 3, jnp.where(kind == TWICE, 2, 0))
        hb = jnp.where(kind >= TWICE, 1, h)
        wk = jnp.concatenate([w[g, ja, h], w[g, jb, hb]], axis=1)
        acc[...] += lax.dot_general(og[k], wk, (((1,), (1,)), ((), ())), preferred_element_type=F32)
        return carry

    def normed_to(k):
        return jnp.clip(NG_RATE * (k - NG_FROM) + 2, 0, k + 1)

    for k in range(LEAD):
        begin(k)

    def slot(s, carry):
        @pl.when((s % 2 == 0) & (s // 2 + LEAD < K))
        def _():
            begin(s // 2 + LEAD)

        for i in range(1, LS):
            k = (s - HOP * i) // 2

            @pl.when((s >= HOP * i) & ((s - HOP * i) % 2 == 0) & (k < K))
            def _(i=i, k=k):
                wait_long(k, i - 1)
                send_long(k, i)
                if i < SS:
                    wait_short(k, i - 1)
                    send_short(k, i)

        @pl.when(s == HOP * LS - 1)
        def _():
            stays[3].wait()
            wait(nb.at[o], c_recv.at[2])
            for i in range(2):
                nt[i * C : (i + 1) * C, :] = nb[i].astype(F32).T.astype(BF)

        @pl.when(s == W_START)
        def _():
            w_start()

        @pl.when(s == W_OWN)
        def _():
            w_far(OWN)

        @pl.when(s == W_Z)
        def _():
            for g in range(OWN):
                wait(w.at[g, 0], wz_recv.at[g])
                w_near(g)

        @pl.when(s == W_FAR)
        def _():
            for g in range(OWN):
                w_far(g)

        @pl.when(s == W_ALL)
        def _():
            for g in range(ZH):
                wait(w.at[g, 2, :, upper], wx_recv.at[g, 2])
                wait(w.at[g, 2, :, lower], wx_recv.at[g, 3])

        @pl.when((s >= HOP * LS) & ((s - HOP * LS) % 2 == 0))
        def _():
            k = (s - HOP * LS) // 2
            gathered(k)
            weight(k)
            lax.fori_loop(normed_to(k - 1), normed_to(k), normed_grad, 0)

        return carry

    lax.fori_loop(0, 2 * (K - 1) + HOP * LS, slot, 0)

    gathered(K - 1)
    lax.fori_loop(normed_to(K - 2), K, normed_grad, 0)
    dns[...] = acc[:, theirs].astype(BF)
    send(dns, dnr, c_send.at[4], c_recv.at[4], partner)
    p = chunk_weight(K - 1)
    for h in range(2):
        total = x_sum(OWN, h, p[:, h * C : (h + 1) * C])
        for i in range(OWN):
            wait(rsz.at[i, h], rsz_recv.at[i, h])
            total = total + rsz[i, h].astype(F32)
        part[K - 1, h] = total.astype(BF)
        fin[:, h * C : (h + 1) * C] = part[K - 1, h, theirs, :]
    send(fin, finr, c_send.at[3], c_recv.at[3], partner)
    for h in range(2):
        dw_ref[:, half(c, h)] = part[K - 1, h, mine, :]
    wait(dnr, c_recv.at[4])
    dn_ref[...] = (acc[:, mine] + dnr[...].astype(F32)).astype(BF)

    wait(og_par, c_send.at[0])
    for h in range(2):
        wait(w.at[OWN, 0, h, mine], c_send.at[5 + h])
    wait(nb.at[0], c_send.at[2])
    wait(fin, c_send.at[3])
    wait(dns, c_send.at[4])
    for q, (first, number) in enumerate(GROUPS):
        wait(og.at[pl.ds(first, number), pl.ds(0, (ZL - 1) * 2 * R)], zl_send.at[q])
    for g in range(OWN):
        wait(w.at[g, 0], wz_send.at[g])
        for h in range(2):
            wait(zs.at[g, h], rsz_send.at[g, h])
    for g in range(ZH):
        wait(w.at[g, 3], wx_send.at[g, 0])
        wait(w.at[g, 1], wx_send.at[g, 1])
        wait(w.at[g, 2, :, upper], wx_send.at[g, 2])
        wait(w.at[g, 2, :, lower], wx_send.at[g, 3])

    for g in range(ZH):
        for h in range(2):
            for i in range(2):
                wait(rsh.at[g, h, i], rs_send.at[g, h, i])
                wait(rsx.at[g, h, i], rs_send.at[g, h, 2 + i])

    def drain(k, carry):
        wait(og.at[k, pl.ds(0, (Y - 1) * B)], y_send.at[k])
        return carry

    lax.fori_loop(0, K, drain, 0)
    wait(finr, c_recv.at[3])
    dw_ref[:, pl.ds(pl.multiple_of(o * W, W), W)] = finr[...]


def body(out_grad, normed, w_out):
    dma = pltpu.SemaphoreType.DMA
    vmem, hbm = pl.BlockSpec(memory_space=pltpu.VMEM), pl.BlockSpec(memory_space=pl.ANY)
    cols = ZH * X * 2 * W
    return pl.pallas_call(
        kernel,
        out_shape=(jax.ShapeDtypeStruct((RT, C), BF), jax.ShapeDtypeStruct((C, 2 * W), BF)),
        in_specs=[hbm] * 3,
        out_specs=(vmem, vmem),
        scratch_shapes=[
            pltpu.VMEM((R, cols), BF),
            pltpu.VMEM((R, cols), BF),
            pltpu.VMEM((K, RT, W), BF),
            pltpu.VMEM((2, RT, C), BF),
            pltpu.VMEM((2 * C, RT), BF),
            pltpu.VMEM((ZH, X, 2, 2 * C, C), BF),
            pltpu.VMEM((K, 2, 2 * C, C), BF),
            pltpu.VMEM((OWN, 2, 2 * C, C), F32),
            pltpu.VMEM((ZH, 2, 2, C, C), BF),
            pltpu.VMEM((ZH, 2, 2, 2 * C, C), BF),
            pltpu.VMEM((OWN, 2, 2 * C, C), BF),
            pltpu.VMEM((OWN, 2, 2 * C, C), BF),
            pltpu.VMEM((C, W), BF),
            pltpu.VMEM((C, W), BF),
            pltpu.VMEM((RT, 2 * C), F32),
            pltpu.VMEM((RT, C), BF),
            pltpu.VMEM((RT, C), BF),
            dma((4,)), dma((7,)), dma((7,)),
            dma((len(GROUPS),)), dma((len(GROUPS),)),
            dma((K,)), dma((K, LS + SS)),
            dma((OWN,)), dma((OWN,)),
            dma((ZH, 4)), dma((ZH, 4)),
            dma((ZH, 2, 4)), dma((ZH, 2, 2)), dma((ZH, 2, 2)),
            dma((OWN, 2)), dma((OWN, 2)),
        ],
        compiler_params=pltpu.CompilerParams(
            collective_id=0, has_side_effects=True, vmem_limit_bytes=44 * 1024 * 1024
        ),
        cost_estimate=pl.CostEstimate(flops=1_600_000_000, bytes_accessed=1_000_000, transcendentals=0),
    )(*(pltpu.with_memory_space_constraint(a, pltpu.HBM) for a in (out_grad, normed, w_out)))


def solution(mesh):
    in_specs = (P(("dp", "tensor"), None), P("dp", "tensor"), P("tensor", "dp"))
    out_specs = (P("dp", "tensor"), P("tensor", "dp"))
    return jax.shard_map(body, mesh=mesh, in_specs=in_specs, out_specs=out_specs, check_vma=False)
```

```python
import jax
import jax.numpy as jnp
from jax import lax
from jax.experimental import pallas as pl
from jax.experimental.pallas import tpu as pltpu
from jax.sharding import PartitionSpec as P

X, ZH, Y, ZL = 4, 3, 8, 4
R = 8
C = 128
W = 2 * C
OWN = ZH - 1
B = 2 * R * ZL
RT = B * Y
LS, SS = Y // 2, Y // 2 - 1
FAR, SIDES, TWICE, HERE = 0, 1, 2, 3
ORDER = [
    (0, FAR, 0), (1, FAR, 0), (0, SIDES, 0), (1, SIDES, 0), (0, FAR, 1), (1, FAR, 1),
    (0, SIDES, 1), (1, SIDES, 1), (2, TWICE, 0), (2, SIDES, 0), (2, SIDES, 1), (2, HERE, 0),
]
K = len(ORDER)
G_TABLE = sum(g << (2 * i) for i, (g, kind, h) in enumerate(ORDER))
KIND_TABLE = sum(kind << (2 * i) for i, (g, kind, h) in enumerate(ORDER))
H_TABLE = sum(h << i for i, (g, kind, h) in enumerate(ORDER))
Z_SLOTS = [(4, 0, 0), (5, 1, 0), (8, 0, 1), (9, 1, 1)]
GROUPS = [(0, 1), (1, 1), (2, 2), (4, 4), (8, 4)]
HOP = 3
LEAD = 1
W_START, W_OWN, W_Z, W_FAR, W_ALL = 7, 12, 17, 22, 25
NG_FROM, NG_RATE = 7, 3
MESH = pl.DeviceIdType.MESH
BF, F32 = jnp.bfloat16, jnp.float32


def pieces(kind, h):
    return {FAR: ((2, h), (0, h)), SIDES: ((1, h), (3, h)), TWICE: ((2, 0), (2, 1)), HERE: ((0, 0), (0, 1))}[kind]


def kernel(
    og_ref, n_ref, w_ref, dn_ref, dw_ref,
    og_own, og_par, og, nb, nt, w, part, kept, rsh, rsx, zs, rsz, fin, finr, acc, dns, dnr,
    own_sem, c_send, c_recv, zl_send, zl_recv, y_send, y_recv, wz_send, wz_recv, wx_send, wx_recv,
    rs_send, rsh_recv, rsx_recv, rsz_send, rsz_recv,
):
    dp, tn = lax.axis_index("dp"), lax.axis_index("tensor")
    zh, x = dp // X, dp % X
    y, zl, c = tn // (2 * ZL), (tn // 2) % ZL, tn % 2
    o = 1 - c
    partner = (dp, tn + 1 - 2 * c)
    zl_peer = [(dp, (y * ZL + (zl + j) % ZL) * 2 + c) for j in range(1, ZL)]
    z_peer = [(((zh + j) % ZH) * X + x, tn) for j in range(1, ZH)]
    x_up, x_down = (zh * X + (x + 1) % X, tn), (zh * X + (x + X - 1) % X, tn)

    def y_peer(sign):
        return (dp, (((y + sign + Y) % Y) * ZL + zl) * 2 + c)

    def send(src, dst, ssem, rsem, to):
        pltpu.make_async_remote_copy(
            src_ref=src, dst_ref=dst, send_sem=ssem, recv_sem=rsem, device_id=to, device_id_type=MESH
        ).start()

    def wait(ref, sem):
        pltpu.make_async_copy(ref, ref, sem).wait()

    mine, theirs = pl.ds(pl.multiple_of(c * C, C), C), pl.ds(pl.multiple_of(o * C, C), C)
    upper, lower = pl.ds(0, C), pl.ds(C, C)

    def half(of, h):
        return pl.ds(pl.multiple_of(of * W + h * C, C), C)

    stays = [
        pltpu.make_async_copy(og_ref, og_own, own_sem.at[0]),
        pltpu.make_async_copy(w_ref.at[:, half(c, 0)], w.at[OWN, 0, 0, mine], own_sem.at[1]),
        pltpu.make_async_copy(w_ref.at[:, half(c, 1)], w.at[OWN, 0, 1, mine], own_sem.at[2]),
        pltpu.make_async_copy(n_ref, nb.at[c], own_sem.at[3]),
    ]
    for copy in stays:
        copy.start()

    barrier = pltpu.get_barrier_semaphore()
    peers = [partner] + zl_peer + [x_up, x_down] + z_peer + [y_peer(1), y_peer(-1)]
    for peer in peers:
        pl.semaphore_signal(barrier, inc=1, device_id=peer, device_id_type=MESH)
    acc[...] = jnp.zeros_like(acc)
    pl.semaphore_wait(barrier, len(peers))

    send(og_ref, og_par, c_send.at[0], c_recv.at[0], partner)
    for h in range(2):
        send(w_ref.at[:, half(o, h)], w.at[OWN, 0, h, mine], c_send.at[5 + h], c_recv.at[5 + h], partner)
    send(n_ref, nb.at[c], c_send.at[2], c_recv.at[2], partner)

    slab = pl.ds(pl.multiple_of((y * ZL + zl) * 2 * R, 2 * R), 2 * R)
    stays[0].wait()
    wait(og_par, c_recv.at[0])
    for q, (first, number) in enumerate(GROUPS):
        for k in range(first, first + number):
            g, kind, h = ORDER[k]
            for i, (j, h) in enumerate(pieces(kind, h)):
                col = ((zh + 1 + g) % ZH * X + (x + j) % X) * 2 * W + c * W + h * C
                col = pl.ds(pl.multiple_of(col, C), C)
                a, b = og_own[:, col].astype(F32), og_par[:, col].astype(F32)
                top, low = jnp.where(c == 0, a, b), jnp.where(c == 0, b, a)
                og[k, slab, i * C : (i + 1) * C] = jnp.concatenate([top, low], axis=0).astype(BF)
        piece = og.at[pl.ds(first, number), slab]
        for peer in zl_peer:
            send(piece, piece, zl_send.at[q], zl_recv.at[q], peer)

    def w_start():
        for h in range(2):
            stays[1 + h].wait()
            wait(w.at[OWN, 0, h, theirs], c_recv.at[5 + h])
        w_near(OWN)
        for j in range(1, ZH):
            g = ZH - 1 - j
            send(w.at[OWN, 0], w.at[g, 0], wz_send.at[g], wz_recv.at[g], z_peer[j - 1])

    def w_near(g):
        send(w.at[g, 0], w.at[g, 3], wx_send.at[g, 0], wx_recv.at[g, 0], x_up)
        send(w.at[g, 0], w.at[g, 1], wx_send.at[g, 1], wx_recv.at[g, 1], x_down)

    def w_far(g):
        wait(w.at[g, 3], wx_recv.at[g, 0])
        send(w.at[g, 3, :, upper], w.at[g, 2, :, upper], wx_send.at[g, 2], wx_recv.at[g, 2], x_up)
        wait(w.at[g, 1], wx_recv.at[g, 1])
        send(w.at[g, 1, :, lower], w.at[g, 2, :, lower], wx_send.at[g, 3], wx_recv.at[g, 3], x_down)

    def block(k, at):
        return og.at[k, pl.ds(pl.multiple_of(((at + 2 * Y) % Y) * B, B), B)]

    def way(k):
        return 1 - 2 * (k % 2)

    def send_long(k, s):
        b = block(k, y - way(k) * s)
        send(b, b, y_send.at[k], y_recv.at[k, s], y_peer(way(k)))

    def send_short(k, s):
        b = block(k, y + way(k) * s)
        send(b, b, y_send.at[k], y_recv.at[k, LS + s], y_peer(-way(k)))

    def wait_long(k, s):
        wait(block(k, y - way(k) * (s + 1)), y_recv.at[k, s])

    def wait_short(k, s):
        wait(block(k, y + way(k) * (s + 1)), y_recv.at[k, LS + s])

    def begin(k):
        for q, (first, number) in enumerate(GROUPS):
            @pl.when(k == first)
            def _():
                wait(og.at[pl.ds(first, number), pl.ds(0, B - 2 * R)], zl_recv.at[q])

        send_long(k, 0)
        send_short(k, 0)

    def gathered(k):
        wait_long(k, LS - 1)
        wait_short(k, SS - 1)

    def chunk_weight(k):
        return jnp.dot(nt[...], og[k], preferred_element_type=F32)

    def x_sum(g, h, total):
        for i in range(2):
            wait(rsx.at[g, h, i], rsx_recv.at[g, h, i])
            total = total + rsx[g, h, i].astype(F32)
        return total

    def weight(k):
        g, kind, h = (G_TABLE >> (2 * k)) & 3, (KIND_TABLE >> (2 * k)) & 3, (H_TABLE >> k) & 1
        p = chunk_weight(k)

        def far(h):
            send(part.at[k, h, upper], rsh.at[g, h, 0], rs_send.at[g, h, 0], rsh_recv.at[g, h, 0], x_up)
            send(part.at[k, h, lower], rsh.at[g, h, 1], rs_send.at[g, h, 1], rsh_recv.at[g, h, 1], x_down)

        @pl.when(kind == FAR)
        def _():
            part[k, h] = p[:, :C].astype(BF)
            far(h)
            kept[g, h] = p[:, C:]

        @pl.when(kind == TWICE)
        def _():
            for i in range(2):
                part[k, i] = p[:, i * C : (i + 1) * C].astype(BF)
            for i in range(2):
                far(i)

        @pl.when(kind == SIDES)
        def _():
            wait(rsh.at[g, h, 0], rsh_recv.at[g, h, 0])
            part[k, 0, :C] = (p[:C, :C] + rsh[g, h, 0].astype(F32)).astype(BF)
            part[k, 0, C:] = p[C:, :C].astype(BF)
            send(part.at[k, 0], rsx.at[g, h, 0], rs_send.at[g, h, 2], rsx_recv.at[g, h, 0], x_up)
            wait(rsh.at[g, h, 1], rsh_recv.at[g, h, 1])
            part[k, 1, :C] = p[:C, C:].astype(BF)
            part[k, 1, C:] = (p[C:, C:] + rsh[g, h, 1].astype(F32)).astype(BF)
            send(part.at[k, 1], rsx.at[g, h, 1], rs_send.at[g, h, 3], rsx_recv.at[g, h, 1], x_down)

        for at, gz, hz in Z_SLOTS:
            @pl.when(k == at)
            def _():
                zs[gz, hz] = x_sum(gz, hz, kept[gz, hz]).astype(BF)
                send(zs.at[gz, hz], rsz.at[gz, hz], rsz_send.at[gz, hz], rsz_recv.at[gz, hz], z_peer[gz])

    def normed_grad(k, carry):
        g, kind, h = (G_TABLE >> (2 * k)) & 3, (KIND_TABLE >> (2 * k)) & 3, (H_TABLE >> k) & 1
        ja = jnp.where(kind == SIDES, 1, jnp.where(kind == HERE, 0, 2))
        jb = jnp.where(kind == SIDES, 3, jnp.where(kind == TWICE, 2, 0))
        hb = jnp.where(kind >= TWICE, 1, h)
        wk = jnp.concatenate([w[g, ja, h], w[g, jb, hb]], axis=1)
        acc[...] += lax.dot_general(og[k], wk, (((1,), (1,)), ((), ())), preferred_element_type=F32)
        return carry

    def normed_to(k):
        return min(max(NG_RATE * (k - NG_FROM) + 2, 0), k + 1)

    for k in range(LEAD):
        begin(k)

    def slot(s):
        @pl.when((s % 2 == 0) & (s // 2 + LEAD < K))
        def _():
            begin(s // 2 + LEAD)

        for i in range(1, LS):
            k = (s - HOP * i) // 2

            @pl.when((s >= HOP * i) & ((s - HOP * i) % 2 == 0) & (k < K))
            def _(i=i, k=k):
                wait_long(k, i - 1)
                send_long(k, i)
                if i < SS:
                    wait_short(k, i - 1)
                    send_short(k, i)

        @pl.when(s == HOP * LS - 1)
        def _():
            stays[3].wait()
            wait(nb.at[o], c_recv.at[2])
            for i in range(2):
                nt[i * C : (i + 1) * C, :] = nb[i].astype(F32).T.astype(BF)

        @pl.when(s == W_START)
        def _():
            w_start()

        @pl.when(s == W_OWN)
        def _():
            w_far(OWN)

        @pl.when(s == W_Z)
        def _():
            for g in range(OWN):
                wait(w.at[g, 0], wz_recv.at[g])
                w_near(g)

        @pl.when(s == W_FAR)
        def _():
            for g in range(OWN):
                w_far(g)

        @pl.when(s == W_ALL)
        def _():
            for g in range(ZH):
                wait(w.at[g, 2, :, upper], wx_recv.at[g, 2])
                wait(w.at[g, 2, :, lower], wx_recv.at[g, 3])

        @pl.when((s >= HOP * LS) & ((s - HOP * LS) % 2 == 0))
        def _():
            k = (s - HOP * LS) // 2
            gathered(k)
            weight(k)
            lax.fori_loop(normed_to(k - 1), normed_to(k), normed_grad, 0)

    for s in range(2 * (K - 1) + HOP * LS):
        slot(s)

    gathered(K - 1)
    lax.fori_loop(normed_to(K - 2), K, normed_grad, 0)
    dns[...] = acc[:, theirs].astype(BF)
    send(dns, dnr, c_send.at[4], c_recv.at[4], partner)
    p = chunk_weight(K - 1)
    for h in range(2):
        total = x_sum(OWN, h, p[:, h * C : (h + 1) * C])
        for i in range(OWN):
            wait(rsz.at[i, h], rsz_recv.at[i, h])
            total = total + rsz[i, h].astype(F32)
        part[K - 1, h] = total.astype(BF)
        fin[:, h * C : (h + 1) * C] = part[K - 1, h, theirs, :]
    send(fin, finr, c_send.at[3], c_recv.at[3], partner)
    for h in range(2):
        dw_ref[:, half(c, h)] = part[K - 1, h, mine, :]
    wait(dnr, c_recv.at[4])
    dn_ref[...] = (acc[:, mine] + dnr[...].astype(F32)).astype(BF)

    wait(og_par, c_send.at[0])
    for h in range(2):
        wait(w.at[OWN, 0, h, mine], c_send.at[5 + h])
    wait(nb.at[0], c_send.at[2])
    wait(fin, c_send.at[3])
    wait(dns, c_send.at[4])
    for q, (first, number) in enumerate(GROUPS):
        wait(og.at[pl.ds(first, number), pl.ds(0, (ZL - 1) * 2 * R)], zl_send.at[q])
    for g in range(OWN):
        wait(w.at[g, 0], wz_send.at[g])
        for h in range(2):
            wait(zs.at[g, h], rsz_send.at[g, h])
    for g in range(ZH):
        wait(w.at[g, 3], wx_send.at[g, 0])
        wait(w.at[g, 1], wx_send.at[g, 1])
        wait(w.at[g, 2, :, upper], wx_send.at[g, 2])
        wait(w.at[g, 2, :, lower], wx_send.at[g, 3])

    for g in range(ZH):
        for h in range(2):
            for i in range(2):
                wait(rsh.at[g, h, i], rs_send.at[g, h, i])
                wait(rsx.at[g, h, i], rs_send.at[g, h, 2 + i])

    def drain(k, carry):
        wait(og.at[k, pl.ds(0, (Y - 1) * B)], y_send.at[k])
        return carry

    lax.fori_loop(0, K, drain, 0)
    wait(finr, c_recv.at[3])
    dw_ref[:, pl.ds(pl.multiple_of(o * W, W), W)] = finr[...]


def body(out_grad, normed, w_out):
    dma = pltpu.SemaphoreType.DMA
    vmem, hbm = pl.BlockSpec(memory_space=pltpu.VMEM), pl.BlockSpec(memory_space=pl.ANY)
    cols = ZH * X * 2 * W
    return pl.pallas_call(
        kernel,
        out_shape=(jax.ShapeDtypeStruct((RT, C), BF), jax.ShapeDtypeStruct((C, 2 * W), BF)),
        in_specs=[hbm] * 3,
        out_specs=(vmem, vmem),
        scratch_shapes=[
            pltpu.VMEM((R, cols), BF),
            pltpu.VMEM((R, cols), BF),
            pltpu.VMEM((K, RT, W), BF),
            pltpu.VMEM((2, RT, C), BF),
            pltpu.VMEM((2 * C, RT), BF),
            pltpu.VMEM((ZH, X, 2, 2 * C, C), BF),
            pltpu.VMEM((K, 2, 2 * C, C), BF),
            pltpu.VMEM((OWN, 2, 2 * C, C), F32),
            pltpu.VMEM((ZH, 2, 2, C, C), BF),
            pltpu.VMEM((ZH, 2, 2, 2 * C, C), BF),
            pltpu.VMEM((OWN, 2, 2 * C, C), BF),
            pltpu.VMEM((OWN, 2, 2 * C, C), BF),
            pltpu.VMEM((C, W), BF),
            pltpu.VMEM((C, W), BF),
            pltpu.VMEM((RT, 2 * C), F32),
            pltpu.VMEM((RT, C), BF),
            pltpu.VMEM((RT, C), BF),
            dma((4,)), dma((7,)), dma((7,)),
            dma((len(GROUPS),)), dma((len(GROUPS),)),
            dma((K,)), dma((K, LS + SS)),
            dma((OWN,)), dma((OWN,)),
            dma((ZH, 4)), dma((ZH, 4)),
            dma((ZH, 2, 4)), dma((ZH, 2, 2)), dma((ZH, 2, 2)),
            dma((OWN, 2)), dma((OWN, 2)),
        ],
        compiler_params=pltpu.CompilerParams(
            collective_id=0, has_side_effects=True, vmem_limit_bytes=44 * 1024 * 1024
        ),
        cost_estimate=pl.CostEstimate(flops=1_600_000_000, bytes_accessed=1_000_000, transcendentals=0),
    )(*(pltpu.with_memory_space_constraint(a, pltpu.HBM) for a in (out_grad, normed, w_out)))


def solution(mesh):
    in_specs = (P(("dp", "tensor"), None), P("dp", "tensor"), P("tensor", "dp"))
    out_specs = (P("dp", "tensor"), P("tensor", "dp"))
    return jax.shard_map(body, mesh=mesh, in_specs=in_specs, out_specs=out_specs, check_vma=False)
```

```python
import jax
import jax.numpy as jnp
from jax import lax
from jax.experimental import pallas as pl
from jax.experimental.pallas import tpu as pltpu
from jax.sharding import PartitionSpec as P

X, ZH, Y, ZL = 4, 3, 8, 4
R = 8
C = 128
W = 2 * C
OWN = ZH - 1
B = 2 * R * ZL
RT = B * Y
LS, SS = Y // 2, Y // 2 - 1
FAR, SIDES, TWICE, HERE = 0, 1, 2, 3
ORDER = [
    (0, FAR, 0), (1, FAR, 0), (0, SIDES, 0), (1, SIDES, 0), (0, FAR, 1), (1, FAR, 1),
    (0, SIDES, 1), (1, SIDES, 1), (2, TWICE, 0), (2, SIDES, 0), (2, SIDES, 1), (2, HERE, 0),
]
K = len(ORDER)
G_TABLE = sum(g << (2 * i) for i, (g, kind, h) in enumerate(ORDER))
KIND_TABLE = sum(kind << (2 * i) for i, (g, kind, h) in enumerate(ORDER))
H_TABLE = sum(h << i for i, (g, kind, h) in enumerate(ORDER))
Z_SLOTS = [(4, 0, 0), (5, 1, 0), (8, 0, 1), (9, 1, 1)]
GROUPS = [(0, 1), (1, 1), (2, 2), (4, 4), (8, 4)]
HOP = 3
LEAD = 2
W_START, W_OWN, W_Z, W_FAR, W_ALL = 7, 12, 17, 22, 25
NG_FROM, NG_RATE = 7, 3
MESH = pl.DeviceIdType.MESH
BF, F32 = jnp.bfloat16, jnp.float32


def pieces(kind, h):
    return {FAR: ((2, h), (0, h)), SIDES: ((1, h), (3, h)), TWICE: ((2, 0), (2, 1)), HERE: ((0, 0), (0, 1))}[kind]


def kernel(
    og_ref, n_ref, w_ref, dn_ref, dw_ref,
    og_own, og_par, og, nb, nt, w, part, kept, rsh, rsx, zs, rsz, fin, finr, acc, dns, dnr,
    own_sem, c_send, c_recv, zl_send, zl_recv, y_send, y_recv, wz_send, wz_recv, wx_send, wx_recv,
    rs_send, rsh_recv, rsx_recv, rsz_send, rsz_recv,
):
    dp, tn = lax.axis_index("dp"), lax.axis_index("tensor")
    zh, x = dp // X, dp % X
    y, zl, c = tn // (2 * ZL), (tn // 2) % ZL, tn % 2
    o = 1 - c
    partner = (dp, tn + 1 - 2 * c)
    zl_peer = [(dp, (y * ZL + (zl + j) % ZL) * 2 + c) for j in range(1, ZL)]
    z_peer = [(((zh + j) % ZH) * X + x, tn) for j in range(1, ZH)]
    x_up, x_down = (zh * X + (x + 1) % X, tn), (zh * X + (x + X - 1) % X, tn)

    def y_peer(sign):
        return (dp, (((y + sign + Y) % Y) * ZL + zl) * 2 + c)

    def send(src, dst, ssem, rsem, to):
        pltpu.make_async_remote_copy(
            src_ref=src, dst_ref=dst, send_sem=ssem, recv_sem=rsem, device_id=to, device_id_type=MESH
        ).start()

    def wait(ref, sem):
        pltpu.make_async_copy(ref, ref, sem).wait()

    mine, theirs = pl.ds(pl.multiple_of(c * C, C), C), pl.ds(pl.multiple_of(o * C, C), C)
    upper, lower = pl.ds(0, C), pl.ds(C, C)

    def half(of, h):
        return pl.ds(pl.multiple_of(of * W + h * C, C), C)

    stays = [
        pltpu.make_async_copy(og_ref, og_own, own_sem.at[0]),
        pltpu.make_async_copy(w_ref.at[:, half(c, 0)], w.at[OWN, 0, 0, mine], own_sem.at[1]),
        pltpu.make_async_copy(w_ref.at[:, half(c, 1)], w.at[OWN, 0, 1, mine], own_sem.at[2]),
        pltpu.make_async_copy(n_ref, nb.at[c], own_sem.at[3]),
    ]
    for copy in stays:
        copy.start()

    barrier = pltpu.get_barrier_semaphore()
    peers = [partner] + zl_peer + [x_up, x_down] + z_peer + [y_peer(1), y_peer(-1)]
    for peer in peers:
        pl.semaphore_signal(barrier, inc=1, device_id=peer, device_id_type=MESH)
    acc[...] = jnp.zeros_like(acc)
    pl.semaphore_wait(barrier, len(peers))

    send(og_ref, og_par, c_send.at[0], c_recv.at[0], partner)
    for h in range(2):
        send(w_ref.at[:, half(o, h)], w.at[OWN, 0, h, mine], c_send.at[5 + h], c_recv.at[5 + h], partner)
    send(n_ref, nb.at[c], c_send.at[2], c_recv.at[2], partner)

    slab = pl.ds(pl.multiple_of((y * ZL + zl) * 2 * R, 2 * R), 2 * R)
    stays[0].wait()
    wait(og_par, c_recv.at[0])
    for q, (first, number) in enumerate(GROUPS):
        for k in range(first, first + number):
            g, kind, h = ORDER[k]
            for i, (j, h) in enumerate(pieces(kind, h)):
                col = ((zh + 1 + g) % ZH * X + (x + j) % X) * 2 * W + c * W + h * C
                col = pl.ds(pl.multiple_of(col, C), C)
                a, b = og_own[:, col].astype(F32), og_par[:, col].astype(F32)
                top, low = jnp.where(c == 0, a, b), jnp.where(c == 0, b, a)
                og[k, slab, i * C : (i + 1) * C] = jnp.concatenate([top, low], axis=0).astype(BF)
        piece = og.at[pl.ds(first, number), slab]
        for peer in zl_peer:
            send(piece, piece, zl_send.at[q], zl_recv.at[q], peer)

    def w_start():
        for h in range(2):
            stays[1 + h].wait()
            wait(w.at[OWN, 0, h, theirs], c_recv.at[5 + h])
        w_near(OWN)
        for j in range(1, ZH):
            g = ZH - 1 - j
            send(w.at[OWN, 0], w.at[g, 0], wz_send.at[g], wz_recv.at[g], z_peer[j - 1])

    def w_near(g):
        send(w.at[g, 0], w.at[g, 3], wx_send.at[g, 0], wx_recv.at[g, 0], x_up)
        send(w.at[g, 0], w.at[g, 1], wx_send.at[g, 1], wx_recv.at[g, 1], x_down)

    def w_far(g):
        wait(w.at[g, 3], wx_recv.at[g, 0])
        send(w.at[g, 3, :, upper], w.at[g, 2, :, upper], wx_send.at[g, 2], wx_recv.at[g, 2], x_up)
        wait(w.at[g, 1], wx_recv.at[g, 1])
        send(w.at[g, 1, :, lower], w.at[g, 2, :, lower], wx_send.at[g, 3], wx_recv.at[g, 3], x_down)

    def block(k, at):
        return og.at[k, pl.ds(pl.multiple_of(((at + 2 * Y) % Y) * B, B), B)]

    def way(k):
        return 1 - 2 * (k % 2)

    def send_long(k, s):
        b = block(k, y - way(k) * s)
        send(b, b, y_send.at[k], y_recv.at[k, s], y_peer(way(k)))

    def send_short(k, s):
        b = block(k, y + way(k) * s)
        send(b, b, y_send.at[k], y_recv.at[k, LS + s], y_peer(-way(k)))

    def wait_long(k, s):
        wait(block(k, y - way(k) * (s + 1)), y_recv.at[k, s])

    def wait_short(k, s):
        wait(block(k, y + way(k) * (s + 1)), y_recv.at[k, LS + s])

    def begin(k):
        for q, (first, number) in enumerate(GROUPS):
            @pl.when(k == first)
            def _():
                wait(og.at[pl.ds(first, number), pl.ds(0, B - 2 * R)], zl_recv.at[q])

        send_long(k, 0)
        send_short(k, 0)

    def gathered(k):
        wait_long(k, LS - 1)
        wait_short(k, SS - 1)

    def chunk_weight(k):
        return jnp.dot(nt[...], og[k], preferred_element_type=F32)

    def x_sum(g, h, total):
        for i in range(2):
            wait(rsx.at[g, h, i], rsx_recv.at[g, h, i])
            total = total + rsx[g, h, i].astype(F32)
        return total

    def weight(k):
        g, kind, h = (G_TABLE >> (2 * k)) & 3, (KIND_TABLE >> (2 * k)) & 3, (H_TABLE >> k) & 1
        p = chunk_weight(k)

        def far(h):
            send(part.at[k, h, upper], rsh.at[g, h, 0], rs_send.at[g, h, 0], rsh_recv.at[g, h, 0], x_up)
            send(part.at[k, h, lower], rsh.at[g, h, 1], rs_send.at[g, h, 1], rsh_recv.at[g, h, 1], x_down)

        @pl.when(kind == FAR)
        def _():
            part[k, h] = p[:, :C].astype(BF)
            far(h)
            kept[g, h] = p[:, C:]

        @pl.when(kind == TWICE)
        def _():
            for i in range(2):
                part[k, i] = p[:, i * C : (i + 1) * C].astype(BF)
            for i in range(2):
                far(i)

        @pl.when(kind == SIDES)
        def _():
            wait(rsh.at[g, h, 0], rsh_recv.at[g, h, 0])
            part[k, 0, :C] = (p[:C, :C] + rsh[g, h, 0].astype(F32)).astype(BF)
            part[k, 0, C:] = p[C:, :C].astype(BF)
            send(part.at[k, 0], rsx.at[g, h, 0], rs_send.at[g, h, 2], rsx_recv.at[g, h, 0], x_up)
            wait(rsh.at[g, h, 1], rsh_recv.at[g, h, 1])
            part[k, 1, :C] = p[:C, C:].astype(BF)
            part[k, 1, C:] = (p[C:, C:] + rsh[g, h, 1].astype(F32)).astype(BF)
            send(part.at[k, 1], rsx.at[g, h, 1], rs_send.at[g, h, 3], rsx_recv.at[g, h, 1], x_down)

        for at, gz, hz in Z_SLOTS:
            @pl.when(k == at)
            def _():
                zs[gz, hz] = x_sum(gz, hz, kept[gz, hz]).astype(BF)
                send(zs.at[gz, hz], rsz.at[gz, hz], rsz_send.at[gz, hz], rsz_recv.at[gz, hz], z_peer[gz])

    def normed_grad(k, carry):
        g, kind, h = (G_TABLE >> (2 * k)) & 3, (KIND_TABLE >> (2 * k)) & 3, (H_TABLE >> k) & 1
        ja = jnp.where(kind == SIDES, 1, jnp.where(kind == HERE, 0, 2))
        jb = jnp.where(kind == SIDES, 3, jnp.where(kind == TWICE, 2, 0))
        hb = jnp.where(kind >= TWICE, 1, h)
        wk = jnp.concatenate([w[g, ja, h], w[g, jb, hb]], axis=1)
        acc[...] += lax.dot_general(og[k], wk, (((1,), (1,)), ((), ())), preferred_element_type=F32)
        return carry

    def normed_to(k):
        return min(max(NG_RATE * (k - NG_FROM) + 2, 0), k + 1)

    for k in range(LEAD):
        begin(k)

    def slot(s):
        @pl.when((s % 2 == 0) & (s // 2 + LEAD < K))
        def _():
            begin(s // 2 + LEAD)

        for i in range(1, LS):
            k = (s - HOP * i) // 2

            @pl.when((s >= HOP * i) & ((s - HOP * i) % 2 == 0) & (k < K))
            def _(i=i, k=k):
                wait_long(k, i - 1)
                send_long(k, i)
                if i < SS:
                    wait_short(k, i - 1)
                    send_short(k, i)

        @pl.when(s == HOP * LS - 1)
        def _():
            stays[3].wait()
            wait(nb.at[o], c_recv.at[2])
            for i in range(2):
                nt[i * C : (i + 1) * C, :] = nb[i].astype(F32).T.astype(BF)

        @pl.when(s == W_START)
        def _():
            w_start()

        @pl.when(s == W_OWN)
        def _():
            w_far(OWN)

        @pl.when(s == W_Z)
        def _():
            for g in range(OWN):
                wait(w.at[g, 0], wz_recv.at[g])
                w_near(g)

        @pl.when(s == W_FAR)
        def _():
            for g in range(OWN):
                w_far(g)

        @pl.when(s == W_ALL)
        def _():
            for g in range(ZH):
                wait(w.at[g, 2, :, upper], wx_recv.at[g, 2])
                wait(w.at[g, 2, :, lower], wx_recv.at[g, 3])

        @pl.when((s >= HOP * LS) & ((s - HOP * LS) % 2 == 0))
        def _():
            k = (s - HOP * LS) // 2
            gathered(k)
            weight(k)
            lax.fori_loop(normed_to(k - 1), normed_to(k), normed_grad, 0)

    for s in range(2 * (K - 1) + HOP * LS):
        slot(s)

    gathered(K - 1)
    lax.fori_loop(normed_to(K - 2), K, normed_grad, 0)
    dns[...] = acc[:, theirs].astype(BF)
    send(dns, dnr, c_send.at[4], c_recv.at[4], partner)
    p = chunk_weight(K - 1)
    for h in range(2):
        total = x_sum(OWN, h, p[:, h * C : (h + 1) * C])
        for i in range(OWN):
            wait(rsz.at[i, h], rsz_recv.at[i, h])
            total = total + rsz[i, h].astype(F32)
        part[K - 1, h] = total.astype(BF)
        fin[:, h * C : (h + 1) * C] = part[K - 1, h, theirs, :]
    send(fin, finr, c_send.at[3], c_recv.at[3], partner)
    for h in range(2):
        dw_ref[:, half(c, h)] = part[K - 1, h, mine, :]
    wait(dnr, c_recv.at[4])
    dn_ref[...] = (acc[:, mine] + dnr[...].astype(F32)).astype(BF)

    wait(og_par, c_send.at[0])
    for h in range(2):
        wait(w.at[OWN, 0, h, mine], c_send.at[5 + h])
    wait(nb.at[0], c_send.at[2])
    wait(fin, c_send.at[3])
    wait(dns, c_send.at[4])
    for q, (first, number) in enumerate(GROUPS):
        wait(og.at[pl.ds(first, number), pl.ds(0, (ZL - 1) * 2 * R)], zl_send.at[q])
    for g in range(OWN):
        wait(w.at[g, 0], wz_send.at[g])
        for h in range(2):
            wait(zs.at[g, h], rsz_send.at[g, h])
    for g in range(ZH):
        wait(w.at[g, 3], wx_send.at[g, 0])
        wait(w.at[g, 1], wx_send.at[g, 1])
        wait(w.at[g, 2, :, upper], wx_send.at[g, 2])
        wait(w.at[g, 2, :, lower], wx_send.at[g, 3])

    for g in range(ZH):
        for h in range(2):
            for i in range(2):
                wait(rsh.at[g, h, i], rs_send.at[g, h, i])
                wait(rsx.at[g, h, i], rs_send.at[g, h, 2 + i])

    def drain(k, carry):
        wait(og.at[k, pl.ds(0, (Y - 1) * B)], y_send.at[k])
        return carry

    lax.fori_loop(0, K, drain, 0)
    wait(finr, c_recv.at[3])
    dw_ref[:, pl.ds(pl.multiple_of(o * W, W), W)] = finr[...]


def body(out_grad, normed, w_out):
    dma = pltpu.SemaphoreType.DMA
    vmem, hbm = pl.BlockSpec(memory_space=pltpu.VMEM), pl.BlockSpec(memory_space=pl.ANY)
    cols = ZH * X * 2 * W
    return pl.pallas_call(
        kernel,
        out_shape=(jax.ShapeDtypeStruct((RT, C), BF), jax.ShapeDtypeStruct((C, 2 * W), BF)),
        in_specs=[hbm] * 3,
        out_specs=(vmem, vmem),
        scratch_shapes=[
            pltpu.VMEM((R, cols), BF),
            pltpu.VMEM((R, cols), BF),
            pltpu.VMEM((K, RT, W), BF),
            pltpu.VMEM((2, RT, C), BF),
            pltpu.VMEM((2 * C, RT), BF),
            pltpu.VMEM((ZH, X, 2, 2 * C, C), BF),
            pltpu.VMEM((K, 2, 2 * C, C), BF),
            pltpu.VMEM((OWN, 2, 2 * C, C), F32),
            pltpu.VMEM((ZH, 2, 2, C, C), BF),
            pltpu.VMEM((ZH, 2, 2, 2 * C, C), BF),
            pltpu.VMEM((OWN, 2, 2 * C, C), BF),
            pltpu.VMEM((OWN, 2, 2 * C, C), BF),
            pltpu.VMEM((C, W), BF),
            pltpu.VMEM((C, W), BF),
            pltpu.VMEM((RT, 2 * C), F32),
            pltpu.VMEM((RT, C), BF),
            pltpu.VMEM((RT, C), BF),
            dma((4,)), dma((7,)), dma((7,)),
            dma((len(GROUPS),)), dma((len(GROUPS),)),
            dma((K,)), dma((K, LS + SS)),
            dma((OWN,)), dma((OWN,)),
            dma((ZH, 4)), dma((ZH, 4)),
            dma((ZH, 2, 4)), dma((ZH, 2, 2)), dma((ZH, 2, 2)),
            dma((OWN, 2)), dma((OWN, 2)),
        ],
        compiler_params=pltpu.CompilerParams(
            collective_id=0, has_side_effects=True, vmem_limit_bytes=44 * 1024 * 1024
        ),
        cost_estimate=pl.CostEstimate(flops=1_600_000_000, bytes_accessed=1_000_000, transcendentals=0),
    )(*(pltpu.with_memory_space_constraint(a, pltpu.HBM) for a in (out_grad, normed, w_out)))


def solution(mesh):
    in_specs = (P(("dp", "tensor"), None), P("dp", "tensor"), P("tensor", "dp"))
    out_specs = (P("dp", "tensor"), P("tensor", "dp"))
    return jax.shard_map(body, mesh=mesh, in_specs=in_specs, out_specs=out_specs, check_vma=False)
```
